32 devices in a mesh: space: 8 (over y, x, core), wshard: 4 (over z).
Axes of the slice: x: 2, y: 2, z: 4, core: 2. Of those that a mesh axis runs over, the one named last changes fastest.
Arguments:
- features: bfloat16 [32, 64, 4096], P('space'), may hold values from -6 to 6
- weights: bfloat16 [27, 128, 64], P(None, 'wshard'), may hold values from -0.15625 to 0.15625
- gain: float32 [128], P('wshard'), may hold values from 0.1 to 1.9
- cotangent: bfloat16 [32, 128, 4096], P('space', 'wshard'), may hold values from -0.015625 to 0.015625
- counts: int32 [8], P('space'), may hold values from 1 to 4, as said below
- neighbors: int32 [32, 26], P('space'), may hold values from -1 to 31, as said below
Outputs:
- activated: bfloat16 [32, 128, 4096], P('space', 'wshard')
- weight_grad: float32 [27, 128, 64], P(None, 'wshard')
- gain_grad: float32 [128], P('wshard')
The draws below stay inside these ranges and needn't reach their ends.
Inputs may be any that keep to these rules, and one draw needn't show every extreme that they name: Slots 0 to counts[s] - 1 of index s hold active tiles. Index s and the index half the space axis away form a pair; of each pair one holds at most 2 tiles and the other more than 3. neighbors[t, d] is the global slot (index of space times 4 plus slot) of the active tile at offset d from tile t, or -1 if there is none or t is inactive; the first offset component is the index of space, so a neighbour at dx lies dx indices away.
All inputs are finite; a program needn't handle non-finite values.
Results may differ from the reference program's by a relative error of at most 0.0035.
Values may be sent and summed in bfloat16 or wider, within the bound.
A program may use at most 128 MiB of HBM per device.

```python
import jax
import jax.numpy as jnp
from jax import lax

TILE = 16
CELLS = 4096
CI = 64
CO = 128
SLOTS = 4
TILES = 32
N_SPACE = 8


offsets = [(along_x, along_y, along_z) for along_x in (-1, 0, 1) for along_y in (-1, 0, 1) for along_z in (-1, 0, 1) if (along_x, along_y, along_z) != (0, 0, 0)]


def tile_layout(key):
    pair_count = N_SPACE // 2
    key_heavy, key_light, key_flip, key_place, key_last = jax.random.split(key, 5)
    share_slots = SLOTS - SLOTS // 4
    heavy_count = jax.random.randint(key_heavy, (pair_count,), share_slots + 1, SLOTS + 1).at[0].set(SLOTS).at[pair_count - 1].set(SLOTS)
    light_count = jax.random.randint(key_light, (pair_count,), 1, SLOTS // 2 + 1).at[0].set(SLOTS // 2)
    flip_bits = jax.random.randint(key_flip, (pair_count,), 0, 2).at[pair_count - 1].set(0)
    counts = jnp.concatenate([jnp.where(flip_bits == 1, heavy_count, light_count), jnp.where(flip_bits == 1, light_count, heavy_count)]).astype(jnp.int32)
    window_cols = SLOTS // 2
    place_keys = jax.random.split(key_place, N_SPACE)
    places = jax.vmap(lambda one_key: jax.random.permutation(one_key, 2 * SLOTS)[:SLOTS])(place_keys).astype(jnp.int32)
    last_places = jax.random.permutation(key_last, SLOTS).astype(jnp.int32)
    places = places.at[N_SPACE - 1].set(last_places)
    row_of = places // window_cols
    col_of = places % window_cols
    active = jnp.arange(SLOTS, dtype=jnp.int32)[None, :] < counts[:, None]
    device_ids = jnp.arange(N_SPACE, dtype=jnp.int32)
    columns = []
    for along_x, along_y, along_z in offsets:
        target = device_ids + along_x
        inside = (target >= 0) & (target < N_SPACE)
        target = jnp.clip(target, 0, N_SPACE - 1)
        want_row = row_of + along_y
        want_col = col_of + along_z
        in_window = (want_row >= 0) & (want_row < 4) & (want_col >= 0) & (want_col < window_cols)
        wanted = want_row * window_cols + want_col
        there_places = places[target]
        live_slots = active[target]
        matches = (there_places[:, None, :] == wanted[:, :, None]) & live_slots[:, None, :]
        found_any = jnp.any(matches, axis=2)
        which_slot = jnp.argmax(matches.astype(jnp.int32), axis=2).astype(jnp.int32)
        global_slot = target[:, None] * SLOTS + which_slot
        is_valid = found_any & in_window & inside[:, None] & active
        columns.append(jnp.where(is_valid, global_slot, -1))
    neighbors = jnp.stack(columns, axis=2).reshape(N_SPACE * SLOTS, 26).astype(jnp.int32)
    return (counts, neighbors)


def draw_counts(key, part):
    counts, neighbors = tile_layout(key)
    return counts


def draw_neighbors(key, part):
    counts, neighbors = tile_layout(key)
    return neighbors


def block_scale(key, shape, cuts, smallest, high):
    factor_of = 1.0
    for position, blocks in cuts:
        draws = jax.random.uniform(jax.random.fold_in(jax.random.fold_in(key, 6), position), (blocks,), jnp.float32, smallest / len(cuts), high / len(cuts))
        factor_of = factor_of * jnp.repeat(jnp.exp(draws), shape[position] // blocks).reshape((-1,) + (1,) * (len(shape) - 1 - position))
    return factor_of


def scatter_about(stream_key, shape, scale, most, cuts=(), kind=jnp.bfloat16):
    entries = scale * jax.random.normal(stream_key, shape, jnp.float32)
    if cuts:
        entries = entries * block_scale(stream_key, shape, cuts, -0.22, 0.18)
    return jnp.clip(entries, -most, most).astype(kind)


def setup_inputs(seed: int = 0) -> dict:
    splits = jax.random.split(jax.random.key(seed), 7)
    features = scatter_about(splits[0], (TILES, CI, CELLS), 1.0, 6.0, ((0, 8),))
    weights = scatter_about(splits[1], (27, CO, CI), (27 * CI) ** -0.5, 0.15625, ((1, 4),))
    gain = jnp.clip(1.0 + 0.18 * jax.random.normal(splits[2], (CO,), jnp.float32), 0.1, 1.9)
    cotangent = scatter_about(splits[3], (TILES, CO, CELLS), ((TILES * CELLS) ** -0.5), 0.015625, ((0, 8), (1, 4)))
    counts = draw_counts(jax.random.fold_in(splits[6], 71), 0)
    neighbors = draw_neighbors(jax.random.fold_in(splits[6], 71), 0)
    return {"features": features, "weights": weights, "gain": gain, "cotangent": cotangent, "counts": counts, "neighbors": neighbors}


offsets = [(along_x, along_y, along_z) for along_x in (-1, 0, 1) for along_y in (-1, 0, 1) for along_z in (-1, 0, 1) if (along_x, along_y, along_z) != (0, 0, 0)]
kernel_offsets = [(along_x, along_y, along_z) for along_x in (-1, 0, 1) for along_y in (-1, 0, 1) for along_z in (-1, 0, 1)]
epsilon = 1e-05

def source_range(step, size):
    if step < 0:
        return slice(size - 1, size)
    if step > 0:
        return slice(0, 1)
    return slice(0, size)

def target_range(step, size):
    if step < 0:
        return slice(0, 1)
    if step > 0:
        return slice(size + 1, size + 2)
    return slice(1, size + 1)

def pad_tiles(tile_cube, neighbors):
    tile_count, channels = (tile_cube.shape[0], tile_cube.shape[1])
    padded = jnp.zeros((tile_count, channels, TILE + 2, TILE + 2, TILE + 2), jnp.bfloat16)
    padded = padded.at[:, :, 1:-1, 1:-1, 1:-1].set(tile_cube)
    for number, (along_x, along_y, along_z) in enumerate(offsets):
        piece = tile_cube[:, :, source_range(along_x, TILE), source_range(along_y, TILE), source_range(along_z, TILE)]
        column = neighbors[:, number]
        taken = jnp.take(piece, jnp.maximum(column, 0).astype(jnp.int32), axis=0)
        taken = jnp.where((column >= 0)[:, None, None, None, None], taken, jnp.zeros_like(taken))
        padded = padded.at[:, :, target_range(along_x, TILE), target_range(along_y, TILE), target_range(along_z, TILE)].set(taken)
    return padded

def block_step(weights, gain, padded, cotangent, active):
    slot_count, channels = (padded.shape[0], padded.shape[1])
    out_rows = weights.shape[1]

    def window(kernel):
        along_x, along_y, along_z = kernel_offsets[kernel]
        part = padded[:, :, 1 + along_x:1 + along_x + TILE, 1 + along_y:1 + along_y + TILE, 1 + along_z:1 + along_z + TILE]
        return part.reshape(slot_count, channels, TILE * TILE * TILE).astype(jnp.float32)
    conv_out = jnp.zeros((slot_count, out_rows, TILE * TILE * TILE), jnp.float32)
    for kernel in range(27):
        conv_out = conv_out + jnp.einsum('oc,scn->son', weights[kernel].astype(jnp.float32), window(kernel), precision=lax.Precision.HIGHEST)
    inv_rms = lax.rsqrt(lax.optimization_barrier(jnp.sum(conv_out * conv_out, axis=1)) / out_rows + epsilon)
    scaled = conv_out * inv_rms[:, None, :]
    normed = scaled * gain[None, :, None]
    mask = active.astype(jnp.float32)[:, None, None]
    activated = (jax.nn.silu(normed) * mask).astype(jnp.bfloat16)
    logistic = jax.nn.sigmoid(normed)
    grad_normed = cotangent.astype(jnp.float32) * logistic * (1.0 + normed * (1.0 - logistic)) * mask
    grad_scaled = grad_normed * gain[None, :, None]
    projection = lax.optimization_barrier(jnp.sum(grad_scaled * scaled, axis=1)) / out_rows
    grad_z = (inv_rms[:, None, :] * (grad_scaled - scaled * projection[:, None, :])).astype(jnp.bfloat16)
    grad_wide = grad_z.astype(jnp.float32)
    weight_part = jnp.stack([jnp.einsum('son,scn->oc', grad_wide, window(kernel), precision=lax.Precision.HIGHEST) for kernel in range(27)])
    gain_part = lax.optimization_barrier(jnp.sum(grad_normed * scaled, axis=(0, 2)))
    return (activated, weight_part, gain_part)

def reference(features, weights, gain, cotangent, counts, neighbors):
    active = jnp.arange(SLOTS, dtype=jnp.int32)[None, :] < counts[:, None]
    flat_active = active.reshape(TILES)
    tile_cube = jnp.where(flat_active[:, None, None], features, jnp.zeros_like(features)).reshape(TILES, CI, TILE, TILE, TILE)
    padded = pad_tiles(tile_cube, neighbors).reshape(N_SPACE, SLOTS, CI, TILE + 2, TILE + 2, TILE + 2)

    def step_block(carry, block):
        weight_sum, gain_sum = carry
        block_pad, block_grad, block_active = block
        activated, weight_part, gain_part = block_step(weights, gain, block_pad, block_grad, block_active)
        return ((weight_sum + weight_part, gain_sum + gain_part), activated)
    initial = (jnp.zeros((27, CO, CI), jnp.float32), jnp.zeros((CO,), jnp.float32))
    blocks = (padded, cotangent.reshape(N_SPACE, SLOTS, CO, CELLS), active)
    (weight_grad, gain_grad), activated = lax.scan(step_block, initial, blocks)
    return (activated.reshape(TILES, CO, CELLS), weight_grad, gain_grad)
```

```python
import functools

import jax
import jax.numpy as jnp
import numpy as np
from jax import lax
from jax.experimental import pallas as pl
from jax.experimental.pallas import tpu as pltpu
from jax.sharding import PartitionSpec as P

TILE = 16
PLANE = TILE * TILE
epsilon = 1e-05
MESH = pl.DeviceIdType.MESH
LANES = 128
BF = jnp.bfloat16
F32 = jnp.float32


def shift_tables():
    perms = np.zeros((9, PLANE, PLANE), np.float32)
    for j in range(9):
        dy, dz = j // 3 - 1, j % 3 - 1
        for y in range(TILE):
            for z in range(TILE):
                source = ((y + dy) % TILE) * TILE + (z + dz) % TILE
                perms[j, source, y * TILE + z] = 1.0
    masks = np.zeros((4, TILE, PLANE), np.float32)
    lane = np.arange(PLANE)
    masks[0] = lane // TILE == 0
    masks[1] = lane // TILE == TILE - 1
    masks[2] = lane % TILE == 0
    masks[3] = lane % TILE == TILE - 1
    return perms, masks


def picked(load, j, masks):
    dy, dz = j // 3 - 1, j % 3 - 1
    value = load(4)
    wide = value.shape
    mask_y = jnp.broadcast_to(masks[0 if dy > 0 else 1][None, :1], wide) > 0
    mask_z = jnp.broadcast_to(masks[2 if dz > 0 else 3][None, :1], wide) > 0
    if dz:
        value = jnp.where(mask_z, load(3 + dz + 1), value)
    if dy:
        beside = load((dy + 1) * 3 + 1)
        if dz:
            beside = jnp.where(mask_z, load(j), beside)
        value = jnp.where(mask_y, beside, value)
    return value


def kernel(
    n_space, n_w, idx, act, feat, w96, gain, cot, perms, masks,
    out, red_out,
    src, edge, sendp, x9, part, conv, sq, inv, pf, pb, ptot, gz, acc, gacc, red, rbuf, full,
    halo_send, halo_recv, sq_send, sq_recv, pb_send, pb_recv, rs_send, rs_recv, ag_send, ag_recv,
):
    slots, channels, _ = feat.shape
    rows_out = cot.shape[1]
    me_s = lax.axis_index("space")
    me_w = lax.axis_index("wshard")
    taps = 9 * channels
    chunk = red.shape[0] // n_space

    barrier = pltpu.get_barrier_semaphore()

    def greet_space(d, c):
        pl.semaphore_signal(
            barrier, inc=1, device_id=(lax.rem(me_s + d, n_space), me_w), device_id_type=MESH
        )
        return c

    def greet_w(d, c):
        pl.semaphore_signal(
            barrier, inc=1, device_id=(me_s, lax.rem(me_w + d, n_w)), device_id_type=MESH
        )
        return c

    lax.fori_loop(1, n_space, greet_space, 0)
    lax.fori_loop(1, n_w, greet_w, 0)

    for s in range(slots):
        sendp[0, s] = feat[s, :, (TILE - 1) * PLANE :]
        sendp[1, s] = feat[s, :, :PLANE]
    pl.semaphore_wait(barrier, n_space - 1 + n_w - 1)

    def halo(side):
        step = 1 if side == 0 else n_space - 1
        return pltpu.make_async_remote_copy(
            src_ref=sendp.at[side],
            dst_ref=edge.at[side, pl.ds(0, slots)],
            send_sem=halo_send.at[side],
            recv_sem=halo_recv.at[side],
            device_id=(lax.rem(me_s + step, n_space), me_w),
            device_id_type=MESH,
        )

    for side in range(2):
        halo(side).start()

    for side in range(2):
        edge[side, slots] = jnp.zeros((channels, PLANE), BF)

    def fill(x, c):
        lanes = pl.ds(pl.multiple_of(x * PLANE, PLANE), PLANE)
        for s in range(slots):
            src[s, x] = feat[s, :, lanes]
        src[slots, x] = jnp.zeros((channels, PLANE), BF)
        return c

    lax.fori_loop(0, TILE, fill, 0)
    acc[...] = jnp.zeros_like(acc)
    gacc[...] = jnp.zeros_like(gacc)

    GROUP = 4

    def inner_cells(t, c):
        for j in range(9):
            def some(g, c, j=j):
                def load(k):
                    return src[idx[t, 9 + k], pl.ds(g * GROUP, GROUP)]

                value = picked(load, j, masks)
                if j != 4:
                    value = jnp.dot(
                        value.reshape(GROUP * channels, PLANE), perms[j], preferred_element_type=F32
                    ).astype(BF).reshape(GROUP, channels, PLANE)
                x9[t, pl.ds(1 + g * GROUP, GROUP), j * channels : (j + 1) * channels] = value
                return c

            lax.fori_loop(0, TILE // GROUP, some, 0)
        return c

    lax.fori_loop(0, slots, inner_cells, 0)

    for side in range(2):
        halo(side).wait()

    def squares(t, d):
        return pltpu.make_async_remote_copy(
            src_ref=sq.at[0, t],
            dst_ref=sq.at[d, t],
            send_sem=sq_send.at[t, d],
            recv_sem=sq_recv.at[t, d],
            device_id=(me_s, lax.rem(me_w + d, n_w)),
            device_id_type=MESH,
        )

    def sums(t, d):
        return pltpu.make_async_remote_copy(
            src_ref=pb.at[0, t],
            dst_ref=pb.at[d, t],
            send_sem=pb_send.at[t, d],
            recv_sem=pb_recv.at[t, d],
            device_id=(me_s, lax.rem(me_w + d, n_w)),
            device_id_type=MESH,
        )

    def forward(t, c):
        for j in range(9):
            values = []
            for side in range(2):
                def load(k, side=side):
                    return edge[side, idx[t, 18 * side + k]][None]

                values.append(picked(load, j, masks))
            value = jnp.concatenate(values, axis=0).reshape(2 * channels, PLANE)
            if j != 4:
                value = jnp.dot(value, perms[j], preferred_element_type=F32).astype(BF)
            x9[t, 0, j * channels : (j + 1) * channels] = value[:channels]
            x9[t, TILE + 1, j * channels : (j + 1) * channels] = value[channels:]

        def layer(x, c):
            part[x] = jnp.dot(w96[...], x9[t, x], preferred_element_type=F32)
            return c

        lax.fori_loop(0, TILE + 2, layer, 0, unroll=2)

        def combine(x, c):
            value = (
                part[x, :rows_out]
                + part[x + 1, rows_out : 2 * rows_out]
                + part[x + 2, 2 * rows_out :]
            )
            conv[t, x] = value
            sq[0, t, pl.ds(x, 1)] = jnp.sum(value * value, axis=0, keepdims=True)
            return c

        lax.fori_loop(0, TILE, combine, 0, unroll=2)
        for d in range(1, n_w):
            squares(t, d).start()
        return c

    lax.fori_loop(0, slots, forward, 0)

    full_rows = rows_out * n_w
    gain_wide = jnp.broadcast_to(gain[...], (rows_out, PLANE))

    def cell_terms(t, x):
        lanes = pl.ds(pl.multiple_of(x * PLANE, PLANE), PLANE)
        row = inv[t, pl.ds(x, 1)]
        scaled = conv[t, x] * row
        normed = scaled * gain_wide
        s = jax.nn.sigmoid(normed)
        grad = cot[t, :, lanes].astype(F32) * s * (1.0 + normed * (1.0 - s)) * act[t]
        return lanes, row, scaled, normed, s, grad

    def middle(t, c):
        for d in range(1, n_w):
            squares(t, d).wait()
        total = sq[0, t]
        for d in range(1, n_w):
            total = total + sq[d, t]
        inv[t] = lax.rsqrt(total / full_rows + epsilon)

        def cells(x, c):
            lanes, row, scaled, normed, s, grad = cell_terms(t, x)
            out[t, :, lanes] = (normed * s * act[t]).astype(BF)
            gacc[...] += grad * scaled
            grad_scaled = grad * gain_wide
            pf[pl.ds(x, 1)] = jnp.sum(grad_scaled * scaled, axis=0, keepdims=True)
            return c

        lax.fori_loop(0, TILE, cells, 0, unroll=2)
        pb[0, t] = pf[...].astype(BF)
        for d in range(1, n_w):
            sums(t, d).start()
        return c

    lax.fori_loop(0, slots, middle, 0)

    for m in (0, 1, TILE + 2, TILE + 3):
        gz[m] = jnp.zeros((rows_out, PLANE), BF)

    def backward(t, c):
        for d in range(1, n_w):
            sums(t, d).wait()
        total = pb[0, t].astype(F32)
        for d in range(1, n_w):
            total = total + pb[d, t].astype(F32)
        ptot[...] = total / full_rows

        def cells(x, c):
            lanes, row, scaled, normed, s, grad = cell_terms(t, x)
            value = row * (grad * gain_wide - scaled * ptot[pl.ds(x, 1)])
            gz[x + 2] = value.astype(BF)
            return c

        lax.fori_loop(0, TILE, cells, 0, unroll=2)

        def layer(x, c):
            left = gz[pl.ds(x, 3)].reshape(3 * rows_out, PLANE)
            acc[...] += lax.dot_general(
                left, x9[t, x], (((1,), (1,)), ((), ())), preferred_element_type=F32
            )
            return c

        lax.fori_loop(0, TILE + 2, layer, 0, unroll=2)
        return c

    lax.fori_loop(0, slots, backward, 0)

    rows = 3 * rows_out
    blocks = (taps + LANES - 1) // LANES
    for b in range(blocks):
        width = min(LANES, taps - b * LANES)
        value = acc[:, b * LANES : b * LANES + width]
        if width < LANES:
            red[b * rows : (b + 1) * rows] = jnp.zeros((rows, LANES), F32)
            red[b * rows : (b + 1) * rows, :width] = value
        else:
            red[b * rows : (b + 1) * rows] = value
    at = blocks * rows
    red[at : at + rows_out] = jnp.broadcast_to(
        jnp.sum(gacc[...], axis=1, keepdims=True), (rows_out, LANES)
    )
    if red.shape[0] > at + rows_out:
        red[at + rows_out :] = jnp.zeros((red.shape[0] - at - rows_out, LANES), F32)

    def piece(ref, index):
        return ref.at[pl.ds(pl.multiple_of(index * chunk, 8), chunk)]

    def scatter(d):
        peer = lax.rem(me_s + d, n_space)
        return pltpu.make_async_remote_copy(
            src_ref=piece(red, peer),
            dst_ref=rbuf.at[d],
            send_sem=rs_send.at[d],
            recv_sem=rs_recv.at[d],
            device_id=(peer, me_w),
            device_id_type=MESH,
        )

    def gather(d, index):
        return pltpu.make_async_remote_copy(
            src_ref=piece(full, index),
            dst_ref=piece(full, index),
            send_sem=ag_send.at[d],
            recv_sem=ag_recv.at[d],
            device_id=(lax.rem(me_s + d, n_space), me_w),
            device_id_type=MESH,
        )

    def each(first):
        def body(d, c):
            first(d)
            return c

        lax.fori_loop(1, n_space, body, 0)

    each(lambda d: scatter(d).start())
    mine = pl.ds(pl.multiple_of(me_s * chunk, 8), chunk)
    rbuf[0] = red[mine]

    def arrived(d):
        scatter(d).wait_recv()
        rbuf[0] += rbuf[d]

    each(arrived)
    full[mine] = rbuf[0]
    each(lambda d: gather(d, me_s).start())
    each(lambda d: gather(d, lax.rem(me_s + n_space - d, n_space)).wait_recv())
    each(lambda d: scatter(d).wait_send())
    each(lambda d: gather(d, me_s).wait_send())
    red_out[...] = full[...]


def shards(features, weights, gain, cotangent, counts, neighbors):
    slots, channels, cells = features.shape
    rows_out = weights.shape[1]
    n_space, n_w = lax.axis_size("space"), lax.axis_size("wshard")
    slot_ids = jnp.arange(slots, dtype=jnp.int32)
    active = slot_ids < counts[0]
    local = jnp.where(neighbors >= 0, neighbors % slots, slots)
    own = jnp.where(active, slot_ids, slots)[:, None]
    idx = jnp.concatenate([local[:, :13], own, local[:, 13:]], axis=1).astype(jnp.int32)
    w96 = weights.reshape(3, 9, rows_out, channels).transpose(0, 2, 1, 3).reshape(
        3 * rows_out, 9 * channels
    )
    perms, masks = shift_tables()
    rows = 3 * rows_out
    blocks = (9 * channels + LANES - 1) // LANES
    used = blocks * rows + rows_out
    red_rows = -(-used // (8 * n_space)) * 8 * n_space
    vmem = pl.BlockSpec(memory_space=pltpu.VMEM)
    smem = pl.BlockSpec(memory_space=pltpu.SMEM)
    dma = pltpu.SemaphoreType.DMA
    out, red = pl.pallas_call(
        functools.partial(kernel, n_space, n_w),
        out_shape=(
            jax.ShapeDtypeStruct((slots, rows_out, cells), BF),
            jax.ShapeDtypeStruct((red_rows, LANES), F32),
        ),
        in_specs=[smem, smem, vmem, vmem, vmem, vmem, vmem, vmem],
        out_specs=(vmem, vmem),
        scratch_shapes=[
            pltpu.VMEM((slots + 1, TILE, channels, PLANE), BF),
            pltpu.VMEM((2, slots + 1, channels, PLANE), BF),
            pltpu.VMEM((2, slots, channels, PLANE), BF),
            pltpu.VMEM((slots, TILE + 2, 9 * channels, PLANE), BF),
            pltpu.VMEM((TILE + 2, rows, PLANE), F32),
            pltpu.VMEM((slots, TILE, rows_out, PLANE), F32),
            pltpu.VMEM((n_w, slots, TILE, PLANE), F32),
            pltpu.VMEM((slots, TILE, PLANE), F32),
            pltpu.VMEM((TILE, PLANE), F32),
            pltpu.VMEM((n_w, slots, TILE, PLANE), BF),
            pltpu.VMEM((TILE, PLANE), F32),
            pltpu.VMEM((TILE + 4, rows_out, PLANE), BF),
            pltpu.VMEM((rows, 9 * channels), F32),
            pltpu.VMEM((rows_out, PLANE), F32),
            pltpu.VMEM((red_rows, LANES), F32),
            pltpu.VMEM((n_space, red_rows // n_space, LANES), F32),
            pltpu.VMEM((red_rows, LANES), F32),
            dma((2,)), dma((2,)),
            dma((slots, n_w)), dma((slots, n_w)),
            dma((slots, n_w)), dma((slots, n_w)),
            dma((n_space,)), dma((n_space,)),
            dma((n_space,)), dma((n_space,)),
        ],
        compiler_params=pltpu.CompilerParams(
            collective_id=0, has_side_effects=True, vmem_limit_bytes=56 * 1024 * 1024
        ),
    )(
        idx, active.astype(F32), features, w96, gain.reshape(rows_out, 1), cotangent,
        jnp.asarray(perms, BF), jnp.asarray(masks, BF),
    )
    taken = red[: blocks * rows].reshape(blocks, 3, rows_out, LANES)[:, ::-1]
    taken = taken.transpose(1, 2, 0, 3).reshape(3, rows_out, blocks * LANES)[:, :, : 9 * channels]
    weight_grad = taken.reshape(3, rows_out, 9, channels).transpose(0, 2, 1, 3).reshape(
        27, rows_out, channels
    )
    gain_grad = red[blocks * rows : blocks * rows + rows_out, 0]
    return (out, weight_grad, gain_grad)


def solution(mesh):
    placed = (
        P("space", None, None),
        P(None, "wshard", None),
        P("wshard"),
        P("space", "wshard", None),
        P("space"),
        P("space", None),
    )
    return jax.shard_map(
        shards,
        mesh=mesh,
        in_specs=placed,
        out_specs=(P("space", "wshard", None), P(None, "wshard", None), P("wshard")),
        check_vma=False,
    )
```

```python
import functools

import jax
import jax.numpy as jnp
import numpy as np
from jax import lax
from jax.experimental import pallas as pl
from jax.experimental.pallas import tpu as pltpu
from jax.sharding import PartitionSpec as P

TILE = 16
PLANE = TILE * TILE
epsilon = 1e-05
MESH = pl.DeviceIdType.MESH
LANES = 128
BF = jnp.bfloat16
F32 = jnp.float32


def shift_tables():
    perms = np.zeros((9, PLANE, PLANE), np.float32)
    for j in range(9):
        dy, dz = j // 3 - 1, j % 3 - 1
        for y in range(TILE):
            for z in range(TILE):
                source = ((y + dy) % TILE) * TILE + (z + dz) % TILE
                perms[j, source, y * TILE + z] = 1.0
    masks = np.zeros((4, TILE, PLANE), np.float32)
    lane = np.arange(PLANE)
    masks[0] = lane // TILE == 0
    masks[1] = lane // TILE == TILE - 1
    masks[2] = lane % TILE == 0
    masks[3] = lane % TILE == TILE - 1
    return perms, masks


def picked(load, j, masks):
    dy, dz = j // 3 - 1, j % 3 - 1
    value = load(4)
    wide = value.shape
    mask_y = jnp.broadcast_to(masks[0 if dy > 0 else 1][None, :1], wide) > 0
    mask_z = jnp.broadcast_to(masks[2 if dz > 0 else 3][None, :1], wide) > 0
    if dz:
        value = jnp.where(mask_z, load(3 + dz + 1), value)
    if dy:
        beside = load((dy + 1) * 3 + 1)
        if dz:
            beside = jnp.where(mask_z, load(j), beside)
        value = jnp.where(mask_y, beside, value)
    return value


def kernel(
    n_space, n_w, neighbors, counts, feat, weights, gain, cot, perms, masks,
    out, weight_out, gain_out,
    w96, src, edge, sendp, x9, part, conv, sq, inv, pf, pb, ptot, gz, acc, gacc, red, rbuf, full,
    halo_send, halo_recv, sq_send, sq_recv, pb_send, pb_recv, rs_send, rs_recv, ag_send, ag_recv,
):
    slots, channels, _ = feat.shape
    rows_out = cot.shape[1]
    me_s = lax.axis_index("space")
    me_w = lax.axis_index("wshard")
    taps = 9 * channels

    def slot(t, k):
        if k == 13:
            return jnp.where(t < counts[0], t, slots)
        found = neighbors[t, k - (k > 13)]
        return jnp.where(found >= 0, lax.rem(found, slots), slots)

    def live(t):
        return jnp.where(t < counts[0], 1.0, 0.0).astype(F32)

    chunk = red.shape[0] // n_space

    barrier = pltpu.get_barrier_semaphore()

    def greet_space(d, c):
        pl.semaphore_signal(
            barrier, inc=1, device_id=(lax.rem(me_s + d, n_space), me_w), device_id_type=MESH
        )
        return c

    def greet_w(d, c):
        pl.semaphore_signal(
            barrier, inc=1, device_id=(me_s, lax.rem(me_w + d, n_w)), device_id_type=MESH
        )
        return c

    lax.fori_loop(1, n_space, greet_space, 0)
    lax.fori_loop(1, n_w, greet_w, 0)

    for s in range(slots):
        sendp[0, s] = feat[s, :, (TILE - 1) * PLANE :]
        sendp[1, s] = feat[s, :, :PLANE]
    pl.semaphore_wait(barrier, n_space - 1 + n_w - 1)

    def halo(side):
        step = 1 if side == 0 else n_space - 1
        return pltpu.make_async_remote_copy(
            src_ref=sendp.at[side],
            dst_ref=edge.at[side, pl.ds(0, slots)],
            send_sem=halo_send.at[side],
            recv_sem=halo_recv.at[side],
            device_id=(lax.rem(me_s + step, n_space), me_w),
            device_id_type=MESH,
        )

    for side in range(2):
        halo(side).start()

    for side in range(2):
        edge[side, slots] = jnp.zeros((channels, PLANE), BF)

    def fill(x, c):
        lanes = pl.ds(pl.multiple_of(x * PLANE, PLANE), PLANE)
        for s in range(slots):
            src[s, x] = feat[s, :, lanes]
        src[slots, x] = jnp.zeros((channels, PLANE), BF)
        return c

    lax.fori_loop(0, TILE, fill, 0)
    for k in range(27):
        dx, j = k // 9, k % 9
        w96[dx * rows_out : (dx + 1) * rows_out, j * channels : (j + 1) * channels] = weights[k]
    acc[...] = jnp.zeros_like(acc)
    gacc[...] = jnp.zeros_like(gacc)

    GROUP = 16

    def inner_cells(t, c):
        for j in range(9):
            def some(g, c, j=j):
                def load(k):
                    return src[slot(t, 9 + k), pl.ds(g * GROUP, GROUP)]

                value = picked(load, j, masks)
                if j != 4:
                    value = jnp.dot(
                        value.reshape(GROUP * channels, PLANE), perms[j], preferred_element_type=F32
                    ).astype(BF).reshape(GROUP, channels, PLANE)
                x9[t, pl.ds(1 + g * GROUP, GROUP), j * channels : (j + 1) * channels] = value
                return c

            lax.fori_loop(0, TILE // GROUP, some, 0)
        return c

    lax.fori_loop(0, slots, inner_cells, 0)

    for side in range(2):
        halo(side).wait()

    for j in range(9):
        values = []
        for t in range(slots):
            for side in range(2):
                def load(k, t=t, side=side):
                    return edge[side, slot(t, 18 * side + k)][None]

                values.append(picked(load, j, masks))
        value = jnp.concatenate(values, axis=0).reshape(2 * slots * channels, PLANE)
        if j != 4:
            value = jnp.dot(value, perms[j], preferred_element_type=F32).astype(BF)
        for t in range(slots):
            for side in range(2):
                start = (2 * t + side) * channels
                x9[t, side * (TILE + 1), j * channels : (j + 1) * channels] = value[
                    start : start + channels
                ]

    def squares(t, d):
        return pltpu.make_async_remote_copy(
            src_ref=sq.at[0, t],
            dst_ref=sq.at[d, t],
            send_sem=sq_send.at[t, d],
            recv_sem=sq_recv.at[t, d],
            device_id=(me_s, lax.rem(me_w + d, n_w)),
            device_id_type=MESH,
        )

    def sums(t, d):
        return pltpu.make_async_remote_copy(
            src_ref=pb.at[0, t],
            dst_ref=pb.at[d, t],
            send_sem=pb_send.at[t, d],
            recv_sem=pb_recv.at[t, d],
            device_id=(me_s, lax.rem(me_w + d, n_w)),
            device_id_type=MESH,
        )

    def forward(t, c):
        def layer(x, c):
            part[x] = jnp.dot(w96[...], x9[t, x], preferred_element_type=F32)
            return c

        lax.fori_loop(0, TILE + 2, layer, 0, unroll=2)

        def combine(x, c):
            value = (
                part[x, :rows_out]
                + part[x + 1, rows_out : 2 * rows_out]
                + part[x + 2, 2 * rows_out :]
            )
            conv[t, x] = value
            sq[0, t, pl.ds(x, 1)] = jnp.sum(value * value, axis=0, keepdims=True)
            return c

        lax.fori_loop(0, TILE, combine, 0, unroll=2)
        for d in range(1, n_w):
            squares(t, d).start()
        return c

    lax.fori_loop(0, slots, forward, 0)

    full_rows = rows_out * n_w
    square = (rows_out, rows_out)
    diagonal = lax.broadcasted_iota(jnp.int32, square, 0) == lax.broadcasted_iota(
        jnp.int32, square, 1
    )
    column = jnp.sum(
        jnp.where(diagonal, jnp.broadcast_to(gain[...], square), 0.0), axis=1, keepdims=True
    )
    gain_wide = jnp.broadcast_to(column, (rows_out, PLANE))

    def cell_terms(t, x):
        lanes = pl.ds(pl.multiple_of(x * PLANE, PLANE), PLANE)
        row = inv[t, pl.ds(x, 1)]
        scaled = conv[t, x] * row
        normed = scaled * gain_wide
        s = jax.nn.sigmoid(normed)
        grad = cot[t, :, lanes].astype(F32) * s * (1.0 + normed * (1.0 - s)) * live(t)
        return lanes, row, scaled, normed, s, grad

    def middle(t, c):
        for d in range(1, n_w):
            squares(t, d).wait()
        total = sq[0, t]
        for d in range(1, n_w):
            total = total + sq[d, t]
        inv[t] = lax.rsqrt(total / full_rows + epsilon)

        def cells(x, c):
            lanes, row, scaled, normed, s, grad = cell_terms(t, x)
            out[t, :, lanes] = (normed * s * live(t)).astype(BF)
            gacc[...] += grad * scaled
            grad_scaled = grad * gain_wide
            pf[pl.ds(x, 1)] = jnp.sum(grad_scaled * scaled, axis=0, keepdims=True)
            return c

        lax.fori_loop(0, TILE, cells, 0, unroll=2)
        pb[0, t] = pf[...].astype(BF)
        for d in range(1, n_w):
            sums(t, d).start()
        return c

    lax.fori_loop(0, slots, middle, 0)

    for m in (0, 1, TILE + 2, TILE + 3):
        gz[m] = jnp.zeros((rows_out, PLANE), BF)

    def backward(t, c):
        for d in range(1, n_w):
            sums(t, d).wait()
        total = pb[0, t].astype(F32)
        for d in range(1, n_w):
            total = total + pb[d, t].astype(F32)
        ptot[...] = total / full_rows

        def cells(x, c):
            lanes, row, scaled, normed, s, grad = cell_terms(t, x)
            value = row * (grad * gain_wide - scaled * ptot[pl.ds(x, 1)])
            gz[x + 2] = value.astype(BF)
            return c

        lax.fori_loop(0, TILE, cells, 0, unroll=2)

        def layer(x, c):
            left = gz[pl.ds(x, 3)].reshape(3 * rows_out, PLANE)
            acc[...] += lax.dot_general(
                left, x9[t, x], (((1,), (1,)), ((), ())), preferred_element_type=F32
            )
            return c

        lax.fori_loop(0, TILE + 2, layer, 0, unroll=2)
        return c

    lax.fori_loop(0, slots, backward, 0)

    rows = 3 * rows_out
    blocks = (taps + LANES - 1) // LANES
    for b in range(blocks):
        width = min(LANES, taps - b * LANES)
        value = acc[:, b * LANES : b * LANES + width]
        if width < LANES:
            red[b * rows : (b + 1) * rows] = jnp.zeros((rows, LANES), F32)
            red[b * rows : (b + 1) * rows, :width] = value
        else:
            red[b * rows : (b + 1) * rows] = value
    at = blocks * rows
    red[at : at + rows_out] = jnp.broadcast_to(
        jnp.sum(gacc[...], axis=1, keepdims=True), (rows_out, LANES)
    )
    if red.shape[0] > at + rows_out:
        red[at + rows_out :] = jnp.zeros((red.shape[0] - at - rows_out, LANES), F32)

    def piece(ref, index):
        return ref.at[pl.ds(pl.multiple_of(index * chunk, 8), chunk)]

    def scatter(d):
        peer = lax.rem(me_s + d, n_space)
        return pltpu.make_async_remote_copy(
            src_ref=piece(red, peer),
            dst_ref=rbuf.at[d],
            send_sem=rs_send.at[d],
            recv_sem=rs_recv.at[d],
            device_id=(peer, me_w),
            device_id_type=MESH,
        )

    def gather(d, index):
        return pltpu.make_async_remote_copy(
            src_ref=piece(full, index),
            dst_ref=piece(full, index),
            send_sem=ag_send.at[d],
            recv_sem=ag_recv.at[d],
            device_id=(lax.rem(me_s + d, n_space), me_w),
            device_id_type=MESH,
        )

    def each(first):
        def body(d, c):
            first(d)
            return c

        lax.fori_loop(1, n_space, body, 0)

    each(lambda d: scatter(d).start())
    mine = pl.ds(pl.multiple_of(me_s * chunk, 8), chunk)
    rbuf[0] = red[mine]

    def arrived(d):
        scatter(d).wait_recv()
        rbuf[0] += rbuf[d]

    each(arrived)
    full[mine] = rbuf[0]
    each(lambda d: gather(d, me_s).start())
    each(lambda d: gather(d, lax.rem(me_s + n_space - d, n_space)).wait_recv())
    each(lambda d: scatter(d).wait_send())
    each(lambda d: gather(d, me_s).wait_send())
    for k in range(27):
        dx, j = k // 9, k % 9
        b, lane = j * channels // LANES, j * channels % LANES
        top = b * rows + (2 - dx) * rows_out
        weight_out[k] = full[top : top + rows_out, lane : lane + channels]
    gain_out[...] = jnp.sum(
        jnp.where(diagonal, full[at : at + rows_out, :rows_out], 0.0), axis=0, keepdims=True
    )


def shards(features, weights, gain, cotangent, counts, neighbors):
    slots, channels, cells = features.shape
    rows_out = weights.shape[1]
    n_space, n_w = lax.axis_size("space"), lax.axis_size("wshard")
    perms, masks = shift_tables()
    rows = 3 * rows_out
    blocks = (9 * channels + LANES - 1) // LANES
    used = blocks * rows + rows_out
    red_rows = -(-used // (8 * n_space)) * 8 * n_space
    vmem = pl.BlockSpec(memory_space=pltpu.VMEM)
    smem = pl.BlockSpec(memory_space=pltpu.SMEM)
    dma = pltpu.SemaphoreType.DMA
    out, weight_grad, gain_grad = pl.pallas_call(
        functools.partial(kernel, n_space, n_w),
        out_shape=(
            jax.ShapeDtypeStruct((slots, rows_out, cells), BF),
            jax.ShapeDtypeStruct((27, rows_out, channels), F32),
            jax.ShapeDtypeStruct((1, rows_out), F32),
        ),
        in_specs=[smem, smem, vmem, vmem, vmem, vmem, vmem, vmem],
        out_specs=(vmem, vmem, vmem),
        scratch_shapes=[
            pltpu.VMEM((rows, 9 * channels), BF),
            pltpu.VMEM((slots + 1, TILE, channels, PLANE), BF),
            pltpu.VMEM((2, slots + 1, channels, PLANE), BF),
            pltpu.VMEM((2, slots, channels, PLANE), BF),
            pltpu.VMEM((slots, TILE + 2, 9 * channels, PLANE), BF),
            pltpu.VMEM((TILE + 2, rows, PLANE), F32),
            pltpu.VMEM((slots, TILE, rows_out, PLANE), F32),
            pltpu.VMEM((n_w, slots, TILE, PLANE), F32),
            pltpu.VMEM((slots, TILE, PLANE), F32),
            pltpu.VMEM((TILE, PLANE), F32),
            pltpu.VMEM((n_w, slots, TILE, PLANE), BF),
            pltpu.VMEM((TILE, PLANE), F32),
            pltpu.VMEM((TILE + 4, rows_out, PLANE), BF),
            pltpu.VMEM((rows, 9 * channels), F32),
            pltpu.VMEM((rows_out, PLANE), F32),
            pltpu.VMEM((red_rows, LANES), F32),
            pltpu.VMEM((n_space, red_rows // n_space, LANES), F32),
            pltpu.VMEM((red_rows, LANES), F32),
            dma((2,)), dma((2,)),
            dma((slots, n_w)), dma((slots, n_w)),
            dma((slots, n_w)), dma((slots, n_w)),
            dma((n_space,)), dma((n_space,)),
            dma((n_space,)), dma((n_space,)),
        ],
        compiler_params=pltpu.CompilerParams(
            collective_id=0, has_side_effects=True, vmem_limit_bytes=56 * 1024 * 1024
        ),
    )(
        neighbors, counts, features, weights, gain.reshape(1, rows_out), cotangent,
        jnp.asarray(perms, BF), jnp.asarray(masks, BF),
    )
    return (out, weight_grad, gain_grad.reshape(rows_out))


def solution(mesh):
    placed = (
        P("space", None, None),
        P(None, "wshard", None),
        P("wshard"),
        P("space", "wshard", None),
        P("space"),
        P("space", None),
    )
    return jax.shard_map(
        shards,
        mesh=mesh,
        in_specs=placed,
        out_specs=(P("space", "wshard", None), P(None, "wshard", None), P("wshard")),
        check_vma=False,
    )
```

```python
import functools

import jax
import jax.numpy as jnp
import numpy as np
from jax import lax
from jax.experimental import pallas as pl
from jax.experimental.pallas import tpu as pltpu
from jax.sharding import PartitionSpec as P

TILE = 16
PLANE = TILE * TILE
epsilon = 1e-05
MESH = pl.DeviceIdType.MESH
LANES = 128
BF = jnp.bfloat16
F32 = jnp.float32


def shift_tables():
    perms = np.zeros((9, PLANE, PLANE), np.float32)
    for j in range(9):
        dy, dz = j // 3 - 1, j % 3 - 1
        for y in range(TILE):
            for z in range(TILE):
                source = ((y + dy) % TILE) * TILE + (z + dz) % TILE
                perms[j, source, y * TILE + z] = 1.0
    masks = np.zeros((4, TILE, PLANE), np.float32)
    lane = np.arange(PLANE)
    masks[0] = lane // TILE == 0
    masks[1] = lane // TILE == TILE - 1
    masks[2] = lane % TILE == 0
    masks[3] = lane % TILE == TILE - 1
    return perms, masks


def picked(load, j, masks):
    dy, dz = j // 3 - 1, j % 3 - 1
    value = load(4)
    wide = value.shape
    mask_y = jnp.broadcast_to(masks[0 if dy > 0 else 1][None, :1], wide) > 0
    mask_z = jnp.broadcast_to(masks[2 if dz > 0 else 3][None, :1], wide) > 0
    if dz:
        value = jnp.where(mask_z, load(3 + dz + 1), value)
    if dy:
        beside = load((dy + 1) * 3 + 1)
        if dz:
            beside = jnp.where(mask_z, load(j), beside)
        value = jnp.where(mask_y, beside, value)
    return value


def kernel(
    n_space, n_w, neighbors, counts, feat, weights, gain, cot, perms, masks,
    out, weight_out, gain_out,
    w96, src, edge, sendp, x9, part, conv, sq, inv, pf, pb, ptot, gz, acc, gacc, red, rbuf, full,
    halo_send, halo_recv, sq_send, sq_recv, pb_send, pb_recv, rs_send, rs_recv, ag_send, ag_recv,
):
    slots, channels, _ = feat.shape
    rows_out = cot.shape[1]
    me_s = lax.axis_index("space")
    me_w = lax.axis_index("wshard")
    taps = 9 * channels

    def slot(t, k):
        if k == 13:
            return jnp.where(t < counts[0], t, slots)
        found = neighbors[t, k - (k > 13)]
        return jnp.where(found >= 0, lax.rem(found, slots), slots)

    def live(t):
        return jnp.where(t < counts[0], 1.0, 0.0).astype(F32)

    chunk = red.shape[0] // n_space

    barrier = pltpu.get_barrier_semaphore()

    def greet_space(d, c):
        pl.semaphore_signal(
            barrier, inc=1, device_id=(lax.rem(me_s + d, n_space), me_w), device_id_type=MESH
        )
        return c

    def greet_w(d, c):
        pl.semaphore_signal(
            barrier, inc=1, device_id=(me_s, lax.rem(me_w + d, n_w)), device_id_type=MESH
        )
        return c

    lax.fori_loop(1, n_space, greet_space, 0)
    lax.fori_loop(1, n_w, greet_w, 0)

    for s in range(slots):
        sendp[0, s] = feat[s, :, (TILE - 1) * PLANE :]
        sendp[1, s] = feat[s, :, :PLANE]

    def halo(side):
        step = 1 if side == 0 else n_space - 1
        return pltpu.make_async_remote_copy(
            src_ref=sendp.at[side],
            dst_ref=edge.at[side, pl.ds(0, slots)],
            send_sem=halo_send.at[side],
            recv_sem=halo_recv.at[side],
            device_id=(lax.rem(me_s + step, n_space), me_w),
            device_id_type=MESH,
        )

    for side in range(2):
        edge[side, slots] = jnp.zeros((channels, PLANE), BF)

    def fill(x, c):
        lanes = pl.ds(pl.multiple_of(x * PLANE, PLANE), PLANE)
        for s in range(slots):
            src[s, x] = feat[s, :, lanes]
        src[slots, x] = jnp.zeros((channels, PLANE), BF)
        return c

    lax.fori_loop(0, TILE, fill, 0)
    for k in range(27):
        dx, j = k // 9, k % 9
        w96[dx * rows_out : (dx + 1) * rows_out, j * channels : (j + 1) * channels] = weights[k]
    acc[...] = jnp.zeros_like(acc)
    gacc[...] = jnp.zeros_like(gacc)

    pl.semaphore_wait(barrier, n_space - 1 + n_w - 1)

    for side in range(2):
        halo(side).start()

    GROUP = 16

    def inner_cells(t, c):
        for j in range(9):
            def some(g, c, j=j):
                def load(k):
                    return src[slot(t, 9 + k), pl.ds(g * GROUP, GROUP)]

                value = picked(load, j, masks)
                if j != 4:
                    value = jnp.dot(
                        value.reshape(GROUP * channels, PLANE), perms[j], preferred_element_type=F32
                    ).astype(BF).reshape(GROUP, channels, PLANE)
                x9[t, pl.ds(1 + g * GROUP, GROUP), j * channels : (j + 1) * channels] = value
                return c

            lax.fori_loop(0, TILE // GROUP, some, 0)
        return c

    lax.fori_loop(0, slots, inner_cells, 0)

    for side in range(2):
        halo(side).wait()

    for j in range(9):
        values = []
        for t in range(slots):
            for side in range(2):
                def load(k, t=t, side=side):
                    return edge[side, slot(t, 18 * side + k)][None]

                values.append(picked(load, j, masks))
        value = jnp.concatenate(values, axis=0).reshape(2 * slots * channels, PLANE)
        if j != 4:
            value = jnp.dot(value, perms[j], preferred_element_type=F32).astype(BF)
        for t in range(slots):
            for side in range(2):
                start = (2 * t + side) * channels
                x9[t, side * (TILE + 1), j * channels : (j + 1) * channels] = value[
                    start : start + channels
                ]

    def squares(t, d):
        return pltpu.make_async_remote_copy(
            src_ref=sq.at[0, t],
            dst_ref=sq.at[d, t],
            send_sem=sq_send.at[t, d],
            recv_sem=sq_recv.at[t, d],
            device_id=(me_s, lax.rem(me_w + d, n_w)),
            device_id_type=MESH,
        )

    def sums(t, d):
        return pltpu.make_async_remote_copy(
            src_ref=pb.at[0, t],
            dst_ref=pb.at[d, t],
            send_sem=pb_send.at[t, d],
            recv_sem=pb_recv.at[t, d],
            device_id=(me_s, lax.rem(me_w + d, n_w)),
            device_id_type=MESH,
        )

    def forward(t, c):
        def layer(x, c):
            part[x] = jnp.dot(w96[...], x9[t, x], preferred_element_type=F32)
            return c

        lax.fori_loop(0, TILE + 2, layer, 0, unroll=6)

        def combine(x, c):
            value = (
                part[x, :rows_out]
                + part[x + 1, rows_out : 2 * rows_out]
                + part[x + 2, 2 * rows_out :]
            )
            conv[t, x] = value
            sq[0, t, pl.ds(x, 1)] = jnp.sum(value * value, axis=0, keepdims=True)
            return c

        lax.fori_loop(0, TILE, combine, 0, unroll=4)
        for d in range(1, n_w):
            squares(t, d).start()
        return c

    lax.fori_loop(0, slots, forward, 0)

    full_rows = rows_out * n_w
    square = (rows_out, rows_out)
    diagonal = lax.broadcasted_iota(jnp.int32, square, 0) == lax.broadcasted_iota(
        jnp.int32, square, 1
    )
    column = jnp.sum(
        jnp.where(diagonal, jnp.broadcast_to(gain[...], square), 0.0), axis=1, keepdims=True
    )
    gain_wide = jnp.broadcast_to(column, (rows_out, PLANE))

    def cell_terms(t, x):
        lanes = pl.ds(pl.multiple_of(x * PLANE, PLANE), PLANE)
        row = inv[t, pl.ds(x, 1)]
        scaled = conv[t, x] * row
        normed = scaled * gain_wide
        s = jax.nn.sigmoid(normed)
        grad = cot[t, :, lanes].astype(F32) * s * (1.0 + normed * (1.0 - s)) * live(t)
        return lanes, row, scaled, normed, s, grad

    def middle(t, c):
        for d in range(1, n_w):
            squares(t, d).wait()
        total = sq[0, t]
        for d in range(1, n_w):
            total = total + sq[d, t]
        inv[t] = lax.rsqrt(total / full_rows + epsilon)

        def cells(x, c):
            lanes, row, scaled, normed, s, grad = cell_terms(t, x)
            out[t, :, lanes] = (normed * s * live(t)).astype(BF)
            gacc[...] += grad * scaled
            grad_scaled = grad * gain_wide
            pf[pl.ds(x, 1)] = jnp.sum(grad_scaled * scaled, axis=0, keepdims=True)
            return c

        lax.fori_loop(0, TILE, cells, 0, unroll=4)
        pb[0, t] = pf[...].astype(BF)
        for d in range(1, n_w):
            sums(t, d).start()
        return c

    lax.fori_loop(0, slots, middle, 0)

    for m in (0, 1, TILE + 2, TILE + 3):
        gz[m] = jnp.zeros((rows_out, PLANE), BF)

    def backward(t, c):
        for d in range(1, n_w):
            sums(t, d).wait()
        total = pb[0, t].astype(F32)
        for d in range(1, n_w):
            total = total + pb[d, t].astype(F32)
        ptot[...] = total / full_rows

        def cells(x, c):
            lanes, row, scaled, normed, s, grad = cell_terms(t, x)
            value = row * (grad * gain_wide - scaled * ptot[pl.ds(x, 1)])
            gz[x + 2] = value.astype(BF)
            return c

        lax.fori_loop(0, TILE, cells, 0, unroll=4)

        def layer(x, c):
            total = None
            for step in range(6):
                left = gz[pl.ds(6 * x + step, 3)].reshape(3 * rows_out, PLANE)
                term = lax.dot_general(
                    left, x9[t, 6 * x + step], (((1,), (1,)), ((), ())), preferred_element_type=F32
                )
                total = term if total is None else total + term
            acc[...] += total
            return c

        lax.fori_loop(0, (TILE + 2) // 6, layer, 0)
        return c

    lax.fori_loop(0, slots, backward, 0)

    rows = 3 * rows_out
    blocks = (taps + LANES - 1) // LANES
    for b in range(blocks):
        width = min(LANES, taps - b * LANES)
        value = acc[:, b * LANES : b * LANES + width]
        if width < LANES:
            red[b * rows : (b + 1) * rows] = jnp.zeros((rows, LANES), F32)
            red[b * rows : (b + 1) * rows, :width] = value
        else:
            red[b * rows : (b + 1) * rows] = value
    at = blocks * rows
    red[at : at + rows_out] = jnp.broadcast_to(
        jnp.sum(gacc[...], axis=1, keepdims=True), (rows_out, LANES)
    )
    if red.shape[0] > at + rows_out:
        red[at + rows_out :] = jnp.zeros((red.shape[0] - at - rows_out, LANES), F32)

    def piece(ref, index):
        return ref.at[pl.ds(pl.multiple_of(index * chunk, 8), chunk)]

    def scatter(d):
        peer = lax.rem(me_s + d, n_space)
        return pltpu.make_async_remote_copy(
            src_ref=piece(red, peer),
            dst_ref=rbuf.at[d],
            send_sem=rs_send.at[d],
            recv_sem=rs_recv.at[d],
            device_id=(peer, me_w),
            device_id_type=MESH,
        )

    def gather(d, index):
        return pltpu.make_async_remote_copy(
            src_ref=piece(full, index),
            dst_ref=piece(full, index),
            send_sem=ag_send.at[d],
            recv_sem=ag_recv.at[d],
            device_id=(lax.rem(me_s + d, n_space), me_w),
            device_id_type=MESH,
        )

    def each(first):
        def body(d, c):
            first(d)
            return c

        lax.fori_loop(1, n_space, body, 0)

    each(lambda d: scatter(d).start())
    mine = pl.ds(pl.multiple_of(me_s * chunk, 8), chunk)
    rbuf[0] = red[mine]

    def arrived(d):
        scatter(d).wait_recv()
        rbuf[0] += rbuf[d]

    each(arrived)
    full[mine] = rbuf[0]
    each(lambda d: gather(d, me_s).start())
    each(lambda d: gather(d, lax.rem(me_s + n_space - d, n_space)).wait_recv())
    each(lambda d: scatter(d).wait_send())
    each(lambda d: gather(d, me_s).wait_send())
    for k in range(27):
        dx, j = k // 9, k % 9
        b, lane = j * channels // LANES, j * channels % LANES
        top = b * rows + (2 - dx) * rows_out
        weight_out[k] = full[top : top + rows_out, lane : lane + channels]
    gain_out[...] = jnp.sum(
        jnp.where(diagonal, full[at : at + rows_out, :rows_out], 0.0), axis=0, keepdims=True
    )


def shards(features, weights, gain, cotangent, counts, neighbors):
    slots, channels, cells = features.shape
    rows_out = weights.shape[1]
    n_space, n_w = lax.axis_size("space"), lax.axis_size("wshard")
    perms, masks = shift_tables()
    rows = 3 * rows_out
    blocks = (9 * channels + LANES - 1) // LANES
    used = blocks * rows + rows_out
    red_rows = -(-used // (8 * n_space)) * 8 * n_space
    vmem = pl.BlockSpec(memory_space=pltpu.VMEM)
    smem = pl.BlockSpec(memory_space=pltpu.SMEM)
    dma = pltpu.SemaphoreType.DMA
    out, weight_grad, gain_grad = pl.pallas_call(
        functools.partial(kernel, n_space, n_w),
        out_shape=(
            jax.ShapeDtypeStruct((slots, rows_out, cells), BF),
            jax.ShapeDtypeStruct((27, rows_out, channels), F32),
            jax.ShapeDtypeStruct((1, rows_out), F32),
        ),
        in_specs=[smem, smem, vmem, vmem, vmem, vmem, vmem, vmem],
        out_specs=(vmem, vmem, vmem),
        scratch_shapes=[
            pltpu.VMEM((rows, 9 * channels), BF),
            pltpu.VMEM((slots + 1, TILE, channels, PLANE), BF),
            pltpu.VMEM((2, slots + 1, channels, PLANE), BF),
            pltpu.VMEM((2, slots, channels, PLANE), BF),
            pltpu.VMEM((slots, TILE + 2, 9 * channels, PLANE), BF),
            pltpu.VMEM((TILE + 2, rows, PLANE), F32),
            pltpu.VMEM((slots, TILE, rows_out, PLANE), F32),
            pltpu.VMEM((n_w, slots, TILE, PLANE), F32),
            pltpu.VMEM((slots, TILE, PLANE), F32),
            pltpu.VMEM((TILE, PLANE), F32),
            pltpu.VMEM((n_w, slots, TILE, PLANE), BF),
            pltpu.VMEM((TILE, PLANE), F32),
            pltpu.VMEM((TILE + 4, rows_out, PLANE), BF),
            pltpu.VMEM((rows, 9 * channels), F32),
            pltpu.VMEM((rows_out, PLANE), F32),
            pltpu.VMEM((red_rows, LANES), F32),
            pltpu.VMEM((n_space, red_rows // n_space, LANES), F32),
            pltpu.VMEM((red_rows, LANES), F32),
            dma((2,)), dma((2,)),
            dma((slots, n_w)), dma((slots, n_w)),
            dma((slots, n_w)), dma((slots, n_w)),
            dma((n_space,)), dma((n_space,)),
            dma((n_space,)), dma((n_space,)),
        ],
        compiler_params=pltpu.CompilerParams(
            collective_id=0, has_side_effects=True, vmem_limit_bytes=56 * 1024 * 1024
        ),
    )(
        neighbors, counts, features, weights, gain.reshape(1, rows_out), cotangent,
        jnp.asarray(perms, BF), jnp.asarray(masks, BF),
    )
    return (out, weight_grad, gain_grad.reshape(rows_out))


def solution(mesh):
    placed = (
        P("space", None, None),
        P(None, "wshard", None),
        P("wshard"),
        P("space", "wshard", None),
        P("space"),
        P("space", None),
    )
    return jax.shard_map(
        shards,
        mesh=mesh,
        in_specs=placed,
        out_specs=(P("space", "wshard", None), P(None, "wshard", None), P("wshard")),
        check_vma=False,
    )
```
